32 devices in a mesh: groups: 2 (over y), tm: 4 (over z), space: 2 (over x), clip: 2 (over core).
Axes of the slice: x: 2, y: 2, z: 4, core: 2. Of those that a mesh axis runs over, the one named last changes fastest.
Arguments:
- latents: bfloat16 [4, 16, 8, 6144], P(('groups', 'clip'), 'tm', 'space'), parts along dimension 0, may hold values from -6 to 6
- frame_counts: int32 [4], P(('groups', 'clip')), parts along dimension 0, may hold values from 2 to 16, as said below
- gain_first: float32 [192], replicated, may hold values from 0.5 to 1.5
- bias_first: float32 [192], replicated, may hold values from -3 to 3
- weight_first: bfloat16 [3, 3, 3, 192, 192], replicated, may hold values from -0.078125 to 0.078125
- gain_second: float32 [192], replicated, may hold values from 0.5 to 1.5
- bias_second: float32 [192], replicated, may hold values from -3 to 3
- weight_second: bfloat16 [3, 3, 3, 192, 192], replicated, may hold values from -0.078125 to 0.078125
Outputs:
- encoded: bfloat16 [4, 16, 8, 6144], P(('groups', 'clip'), 'tm', 'space'), parts along dimension 0
The draws below stay inside these ranges and needn't reach their ends.
There are 2 independent parts, one for each index of `groups`. The reference program is written for one: setup_inputs(seed, part) draws one part's arguments, and reference() takes and returns one part's arrays. A program takes and returns all parts, laid end to end along the dimension named above; an argument that names none is the same for every part. Nothing has to cross between parts.
Inputs may be any that keep to these rules, and one draw needn't show every extreme that they name: `frame_counts`: in every part exactly one clip has all 16 frames valid; every other clip has fewer.
All inputs are finite; a program needn't handle non-finite values.
Results may differ from the reference program's by a relative error of at most 0.007.
Values may be sent and summed in bfloat16 or wider, within the bound.
A program may use at most 64 MiB of HBM per device.

```python
import jax
import jax.numpy as jnp
from jax import lax

C = 192
COLS = 32
CLIPS = 2
FRAMES = 16
ROWS = 8


def draw_frame_counts(key, part):
    count_key = jax.random.fold_in(key, 11)
    pick_key = jax.random.fold_in(key, 23)
    drawn = jax.random.randint(count_key, (CLIPS,), 2, FRAMES)
    full_clip = jax.random.randint(pick_key, (), 0, CLIPS)
    return jnp.where(jnp.arange(CLIPS, dtype=jnp.int32) == full_clip, FRAMES, drawn).astype(jnp.int32)


def level_of(key, dims, shards, smallest, largest):
    level = 1.0
    for axis_at, blocks in shards:
        draws = jax.random.uniform(jax.random.fold_in(jax.random.fold_in(key, 6), axis_at), (blocks,), jnp.float32, smallest / len(shards), largest / len(shards))
        level = level * jnp.repeat(jnp.exp(draws), dims[axis_at] // blocks).reshape((-1,) + (1,) * (len(dims) - 1 - axis_at))
    return level


def noise(own_key, extent, deviation, most, pieces=(), kind=jnp.bfloat16):
    values = deviation * jax.random.normal(own_key, extent, jnp.float32)
    if pieces:
        values = values * level_of(own_key, extent, pieces, -0.22, 0.18)
    return jnp.clip(values, -most, most).astype(kind)


def setup_inputs(seed: int = 0, part: int = 0) -> dict:
    splits = jax.random.split(jax.random.key(seed), 9)
    part_splits = jax.random.split(jax.random.fold_in(splits[8], part), 9)
    latents = noise(part_splits[0], (CLIPS, FRAMES, ROWS, COLS * C), 1.0, 6.0, ((0, 2), (1, 4), (2, 2)))
    frame_counts = draw_frame_counts(jax.random.fold_in(jax.random.fold_in(splits[8], part), 71), part)
    gain_first = jnp.clip(jax.random.uniform(splits[2], (C,), jnp.float32, 0.5, 1.5), 0.5, 1.5)
    bias_first = noise(splits[3], (C,), 0.5, 3.0, (), jnp.float32)
    weight_first = noise(splits[4], (3, 3, 3, C, C), (27 * C) ** -0.5, 0.078125)
    gain_second = jnp.clip(jax.random.uniform(splits[5], (C,), jnp.float32, 0.5, 1.5), 0.5, 1.5)
    bias_second = noise(splits[6], (C,), 0.5, 3.0, (), jnp.float32)
    weight_second = noise(splits[7], (3, 3, 3, C, C), (27 * C) ** -0.5, 0.078125)
    return dict(latents=latents, frame_counts=frame_counts, gain_first=gain_first, bias_first=bias_first, weight_first=weight_first, gain_second=gain_second, bias_second=bias_second, weight_second=weight_second)


def norm_silu(values, gain):
    values = values.astype(jnp.float32)
    mean_square = lax.optimization_barrier(jnp.mean(values * values, axis=-1, keepdims=True))
    scaled = values * lax.rsqrt(mean_square + 1e-06) * gain
    return jax.nn.silu(scaled).astype(jnp.bfloat16)

def causal_conv(inputs, kernel):
    return lax.conv_general_dilated(inputs.astype(jnp.float32), kernel.astype(jnp.float32), (1, 1, 1), ((2, 0), (1, 1), (1, 1)), dimension_numbers=('NDHWC', 'DHWIO', 'NDHWC'), precision=lax.Precision.HIGHEST)

def reference(latents, frame_counts, gain_first, bias_first, weight_first, gain_second, bias_second, weight_second):
    channels = gain_first.shape[0]
    clips, frames, rows, flat_width = latents.shape
    shaped = latents.reshape(clips, frames, rows, flat_width // channels, channels)
    frame_index = jnp.arange(frames, dtype=jnp.int32)
    valid = frame_index[None, :] < frame_counts[:, None]
    frame_mask = valid[:, :, None, None, None]
    masked_input = jnp.where(frame_mask, shaped, jnp.zeros_like(shaped))
    normed_first = norm_silu(masked_input, gain_first)
    hidden_first = jnp.where(frame_mask, causal_conv(normed_first, weight_first) + bias_first, 0.0).astype(jnp.bfloat16)
    normed_second = norm_silu(hidden_first, gain_second)
    summed = masked_input.astype(jnp.float32) + causal_conv(normed_second, weight_second) + bias_second
    encoded = jnp.where(frame_mask, summed, 0.0).astype(jnp.bfloat16)
    return encoded.reshape(clips, frames, rows, flat_width)
```

```python
import functools

import jax
import jax.numpy as jnp
from jax import lax
from jax.experimental import pallas as pl
from jax.experimental.pallas import tpu as pltpu
from jax.sharding import PartitionSpec as P

MESH = pl.DeviceIdType.MESH
WIDE = 256


def pair_norm(values, valid, gain):
    channels = gain.shape[-1]
    mean_square = jnp.sum(values * values, axis=-1, keepdims=True) * (1.0 / channels)
    scaled = values * lax.rsqrt(mean_square + 1e-06) * gain
    out = scaled * jax.nn.sigmoid(scaled)
    return jnp.where(valid, out, 0.0)


def split_pair(flat, channels):
    return flat[..., :channels], flat[..., channels:]


def kernel(
    bands,
    blocks,
    counts_ref,
    x_ref,
    gain1_ref,
    bias1_ref,
    gain2_ref,
    bias2_ref,
    w1_ref,
    w2_ref,
    out_ref,
    w1,
    w2,
    p1,
    p2,
    from_time,
    from_space,
    from_corner,
    hidden_out,
    hidden_in,
    w_sems,
    send_sems,
    recv_sems,
):
    frames, rows, pairs, flat = x_ref.shape
    channels = flat // 2
    sides = 1 if bands == 2 else 2
    extra = sides
    hrows = rows + extra
    tm = lax.axis_index("tm")
    band = lax.axis_index("space")
    has_prev = tm > 0
    has_next = tm < blocks - 1
    count = counts_ref[0]
    if sides == 1:
        other = 1 - band
        links = [(other, None, other * (rows - 2), 0)]
        own_at = 1 + band
        slot_at = [(1 - band) * (rows + 1)]
        hidden_at = 1 - band
    else:
        links = [
            (band - 1, band > 0, 0, 1),
            (band + 1, band < bands - 1, rows - 2, 0),
        ]
        own_at = 2
        slot_at = [0, rows + 2]
        hidden_at = 0

    def both(a, b):
        return b if a is None else (a if b is None else jnp.logical_and(a, b))

    def when(cond, fn):
        if cond is None:
            fn()
        else:
            pl.when(cond)(fn)

    peers = [({"space": p}, c) for p, c, _, _ in links]
    for step, has in ((1, has_next), (-1, has_prev)):
        peers.append(({"tm": tm + step}, has))
        peers += [({"tm": tm + step, "space": p}, both(c, has)) for p, c, _, _ in links]

    barrier = pltpu.get_barrier_semaphore()
    total = 0
    for device, cond in peers:
        when(
            cond,
            lambda device=device: pl.semaphore_signal(
                barrier, inc=1, device_id=device, device_id_type=MESH
            ),
        )
        total = total + (1 if cond is None else cond.astype(jnp.int32))

    load1 = pltpu.make_async_copy(w1_ref, w1.at[:, pl.ds(0, channels)], w_sems.at[0])
    load2 = pltpu.make_async_copy(w2_ref, w2.at[:, pl.ds(0, channels)], w_sems.at[1])
    load1.start()
    load2.start()

    pl.semaphore_wait(barrier, total)

    tail = pl.ds(frames - 2, 2)
    copies = []

    def remote(src, dst, at, device, send_if, recv_if):
        copy = pltpu.make_async_remote_copy(
            src_ref=src,
            dst_ref=dst,
            send_sem=send_sems.at[at],
            recv_sem=recv_sems.at[at],
            device_id=device,
            device_id_type=MESH,
        )
        return copy, send_if, recv_if

    slot_cond = [None] if sides == 1 else [band > 0, band < bands - 1]
    space_copies, corner_copies = [], []
    for peer, cond, edge, slot in links:
        space_copies.append(
            remote(
                x_ref.at[:, pl.ds(edge, 2)], from_space.at[slot], slot, {"space": peer}, cond, None
            )
        )
        corner_copies.append(
            remote(
                x_ref.at[tail, pl.ds(edge, 2)],
                from_corner.at[slot],
                2 + slot,
                {"tm": tm + 1, "space": peer},
                both(cond, has_next),
                None,
            )
        )
    time_copy = remote(x_ref.at[tail], from_time, 4, {"tm": tm + 1}, has_next, has_prev)
    hidden_copy = remote(hidden_out, hidden_in, 5, {"tm": tm + 1}, has_next, has_prev)
    for copy, cond, _ in space_copies + [time_copy] + corner_copies:
        when(cond, copy.start)

    p1[...] = jnp.zeros_like(p1)
    p2[...] = jnp.zeros_like(p2)
    spare = WIDE - channels
    w1[:, channels:] = jnp.zeros((w1.shape[0], spare, channels), w1.dtype)
    w2[:, channels:] = jnp.zeros((w2.shape[0], spare, channels), w2.dtype)

    first = tm * frames
    pair_index = lax.broadcasted_iota(jnp.int32, (1, 1, pairs, 1), 2)

    def put(planes, even, odd, frame_at, row_at):
        nf, nr = even.shape[:2]
        before = jnp.where(pair_index > 0, pltpu.roll(odd, 1, 2), 0.0)
        after = jnp.where(pair_index < pairs - 1, pltpu.roll(even, pairs - 1, 2), 0.0)
        for plane, values in enumerate((before, even, odd, after)):
            planes[plane, pl.ds(frame_at, nf), pl.ds(row_at, nr), :, pl.ds(0, channels)] = (
                values.astype(planes.dtype)
            )

    def frame_valid(shape, frame_at):
        index = first - 2 + frame_at + lax.broadcasted_iota(jnp.int32, shape, 0)
        return index < count

    def put_input(raw, frame_at, row_at):
        nf, nr = raw.shape[:2]
        even, odd = split_pair(raw.astype(jnp.float32), channels)
        valid = frame_valid((nf, 1, 1, 1), frame_at)
        gain = gain1_ref[...].reshape(1, 1, 1, channels)
        put(p1, pair_norm(even, valid, gain), pair_norm(odd, valid, gain), frame_at, row_at)

    def conv(planes, w, frame_at, nf, nr):
        total = None
        for a in range(3):
            for b in range(3):
                for e in range(3):
                    patch = planes[
                        e : e + 2, frame_at + a : frame_at + a + nf, b : b + nr
                    ].reshape(2 * nf * nr * pairs, WIDE)
                    term = jnp.dot(
                        patch, w[(a * 3 + b) * 3 + e], preferred_element_type=jnp.float32
                    )
                    total = term if total is None else total + term
        return total.reshape(2, nf, nr, pairs, channels)

    def hidden(frame_at, nf):
        summed = conv(p1, w1, frame_at, nf, hrows) + bias1_ref[...].reshape(1, 1, 1, 1, channels)
        valid = frame_valid((nf, 1, 1, 1), frame_at + 2)
        if sides == 2:
            row = band * rows - 1 + lax.broadcasted_iota(jnp.int32, (1, hrows, 1, 1), 1)
            valid = valid & (row >= 0) & (row < bands * rows)
        rounded = summed.astype(jnp.bfloat16).astype(jnp.float32)
        gain = gain2_ref[...].reshape(1, 1, 1, channels)
        even = pair_norm(rounded[0], valid, gain)
        odd = pair_norm(rounded[1], valid, gain)
        put(p2, even, odd, frame_at + 2, hidden_at)
        return even, odd

    def finish(frame_at, nf):
        summed = conv(p2, w2, frame_at, nf, rows) + bias2_ref[...].reshape(1, 1, 1, 1, channels)
        joined = jnp.concatenate([summed[0], summed[1]], axis=-1)
        added = joined + x_ref[pl.ds(frame_at, nf)].astype(jnp.float32)
        valid = frame_valid((nf, 1, 1, 1), frame_at + 2)
        out_ref[pl.ds(frame_at, nf)] = jnp.where(valid, added, 0.0).astype(out_ref.dtype)

    put_input(x_ref[...], 2, own_at)
    for slot, (copy, _, _) in enumerate(space_copies):

        def arrived(slot=slot):
            landed = remote(
                x_ref.at[:, pl.ds(0, 2)], from_space.at[slot], slot, {"space": band}, None, None
            )[0]
            landed.wait_recv()
            put_input(from_space[slot], 2, slot_at[slot])

        when(slot_cond[slot], arrived)

    load1.wait()
    even, odd = hidden(frames - 2, 2)
    hidden_out[0] = even.astype(hidden_out.dtype)
    hidden_out[1] = odd.astype(hidden_out.dtype)
    when(has_next, hidden_copy[0].start)

    def time_arrived():
        time_copy[0].wait_recv()
        put_input(from_time[...], 0, own_at)

    when(has_prev, time_arrived)
    for slot in range(sides):

        def corner_arrived(slot=slot):
            landed = remote(
                x_ref.at[tail, pl.ds(0, 2)],
                from_corner.at[slot],
                2 + slot,
                {"space": band},
                None,
                None,
            )[0]
            landed.wait_recv()
            put_input(from_corner[slot], 0, slot_at[slot])

        when(both(slot_cond[slot], has_prev), corner_arrived)

    hidden(0, frames - 2)
    load2.wait()
    finish(frames - 2, 2)

    def hidden_arrived():
        hidden_copy[0].wait_recv()
        even = hidden_in[0].astype(jnp.float32)
        odd = hidden_in[1].astype(jnp.float32)
        put(p2, even, odd, 0, hidden_at)

    when(has_prev, hidden_arrived)
    finish(0, frames - 2)
    for copy, cond, _ in space_copies + corner_copies + [time_copy, hidden_copy]:
        when(cond, copy.wait_send)


def shards(
    bands,
    blocks,
    latents,
    frame_counts,
    gain_first,
    bias_first,
    weight_first,
    gain_second,
    bias_second,
    weight_second,
):
    channels = gain_first.shape[0]
    frames, rows, flat_width = latents.shape[1:]
    pairs = flat_width // (2 * channels)
    x = latents.reshape(frames, rows, pairs, 2 * channels)
    sides = 1 if bands == 2 else 2
    hrows = rows + sides
    bf16 = jnp.bfloat16
    vmem = pl.BlockSpec(memory_space=pltpu.VMEM)
    hbm = pl.BlockSpec(memory_space=pl.ANY)
    out = pl.pallas_call(
        functools.partial(kernel, bands, blocks),
        out_shape=jax.ShapeDtypeStruct(x.shape, bf16),
        in_specs=[pl.BlockSpec(memory_space=pltpu.SMEM)] + [vmem] * 5 + [hbm] * 2,
        out_specs=vmem,
        scratch_shapes=[
            pltpu.VMEM((27, WIDE, channels), bf16),
            pltpu.VMEM((27, WIDE, channels), bf16),
            pltpu.VMEM((4, frames + 2, hrows + 2, pairs, WIDE), bf16),
            pltpu.VMEM((4, frames + 2, rows + 2, pairs, WIDE), bf16),
            pltpu.VMEM((2, rows, pairs, 2 * channels), bf16),
            pltpu.VMEM((sides, frames, 2, pairs, 2 * channels), bf16),
            pltpu.VMEM((sides, 2, 2, pairs, 2 * channels), bf16),
            pltpu.VMEM((2, 2, hrows, pairs, channels), bf16),
            pltpu.VMEM((2, 2, hrows, pairs, channels), bf16),
            pltpu.SemaphoreType.DMA((2,)),
            pltpu.SemaphoreType.DMA((6,)),
            pltpu.SemaphoreType.DMA((6,)),
        ],
        compiler_params=pltpu.CompilerParams(
            collective_id=0, has_side_effects=True, vmem_limit_bytes=40 * 1024 * 1024
        ),
    )(
        frame_counts,
        x,
        gain_first.reshape(1, channels),
        bias_first.reshape(1, channels),
        gain_second.reshape(1, channels),
        bias_second.reshape(1, channels),
        weight_first.reshape(27, channels, channels),
        weight_second.reshape(27, channels, channels),
    )
    return out.reshape(latents.shape)


def solution(mesh):
    return jax.shard_map(
        functools.partial(shards, mesh.shape["space"], mesh.shape["tm"]),
        mesh=mesh,
        in_specs=(P(("groups", "clip"), "tm", "space", None), P(("groups", "clip"))) + (P(),) * 6,
        out_specs=P(("groups", "clip"), "tm", "space", None),
        check_vma=False,
    )
```

```python
import functools

import jax
import jax.numpy as jnp
from jax import lax
from jax.experimental import pallas as pl
from jax.experimental.pallas import tpu as pltpu
from jax.sharding import PartitionSpec as P

MESH = pl.DeviceIdType.MESH
WIDE = 256


def pair_norm(values, valid, gain):
    channels = gain.shape[-1]
    mean_square = jnp.sum(values * values, axis=-1, keepdims=True) * (1.0 / channels)
    scaled = values * lax.rsqrt(mean_square + 1e-06) * gain
    out = scaled * jax.nn.sigmoid(scaled)
    return jnp.where(valid, out, 0.0)


def split_pair(flat, channels):
    return flat[..., :channels], flat[..., channels:]


def kernel(
    bands,
    blocks,
    counts_ref,
    x_ref,
    gain1_hbm,
    bias1_hbm,
    gain2_hbm,
    bias2_hbm,
    w1_ref,
    w2_ref,
    out_ref,
    vectors,
    w1,
    w2,
    p1,
    p2,
    from_time,
    from_space,
    from_corner,
    hidden_out,
    hidden_in,
    w_sems,
    send_sems,
    recv_sems,
):
    frames, rows, pairs, flat = x_ref.shape
    channels = flat // 2
    sides = 1 if bands == 2 else 2
    extra = sides
    hrows = rows + extra
    tm = lax.axis_index("tm")
    band = lax.axis_index("space")
    has_prev = tm > 0
    has_next = tm < blocks - 1
    count = counts_ref[0]
    if sides == 1:
        other = 1 - band
        links = [(other, None, other * (rows - 2), 0)]
        own_at = 1 + band
        slot_at = [(1 - band) * (rows + 1)]
        hidden_at = 1 - band
    else:
        links = [
            (band - 1, band > 0, 0, 1),
            (band + 1, band < bands - 1, rows - 2, 0),
        ]
        own_at = 2
        slot_at = [0, rows + 2]
        hidden_at = 0

    def both(a, b):
        return b if a is None else (a if b is None else jnp.logical_and(a, b))

    def when(cond, fn):
        if cond is None:
            fn()
        else:
            pl.when(cond)(fn)

    peers = [({"space": p}, c) for p, c, _, _ in links]
    for step, has in ((1, has_next), (-1, has_prev)):
        peers.append(({"tm": tm + step}, has))
        peers += [({"tm": tm + step, "space": p}, both(c, has)) for p, c, _, _ in links]

    barrier = pltpu.get_barrier_semaphore()
    total = 0
    for device, cond in peers:
        when(
            cond,
            lambda device=device: pl.semaphore_signal(
                barrier, inc=1, device_id=device, device_id_type=MESH
            ),
        )
        total = total + (1 if cond is None else cond.astype(jnp.int32))

    load1 = pltpu.make_async_copy(w1_ref, w1.at[:, pl.ds(0, channels)], w_sems.at[0])
    load2 = pltpu.make_async_copy(w2_ref, w2.at[:, pl.ds(0, channels)], w_sems.at[1])
    small = [
        pltpu.make_async_copy(source, vectors.at[i], w_sems.at[2 + i])
        for i, source in enumerate((gain1_hbm, bias1_hbm, gain2_hbm, bias2_hbm))
    ]
    gain1_ref, bias1_ref, gain2_ref, bias2_ref = [vectors.at[i] for i in range(4)]
    for copy in small:
        copy.start()
    load1.start()
    load2.start()

    pl.semaphore_wait(barrier, total)

    tail = pl.ds(frames - 2, 2)
    copies = []

    def remote(src, dst, at, device, send_if, recv_if):
        copy = pltpu.make_async_remote_copy(
            src_ref=src,
            dst_ref=dst,
            send_sem=send_sems.at[at],
            recv_sem=recv_sems.at[at],
            device_id=device,
            device_id_type=MESH,
        )
        return copy, send_if, recv_if

    slot_cond = [None] if sides == 1 else [band > 0, band < bands - 1]
    space_copies, corner_copies = [], []
    for peer, cond, edge, slot in links:
        space_copies.append(
            remote(
                x_ref.at[:, pl.ds(edge, 2)], from_space.at[slot], slot, {"space": peer}, cond, None
            )
        )
        corner_copies.append(
            remote(
                x_ref.at[tail, pl.ds(edge, 2)],
                from_corner.at[slot],
                2 + slot,
                {"tm": tm + 1, "space": peer},
                both(cond, has_next),
                None,
            )
        )
    time_copy = remote(x_ref.at[tail], from_time, 4, {"tm": tm + 1}, has_next, has_prev)
    hidden_copy = remote(hidden_out, hidden_in, 5, {"tm": tm + 1}, has_next, has_prev)
    for copy, cond, _ in space_copies + [time_copy] + corner_copies:
        when(cond, copy.start)

    p1[...] = jnp.zeros_like(p1)
    p2[...] = jnp.zeros_like(p2)
    spare = WIDE - channels
    w1[:, channels:] = jnp.zeros((w1.shape[0], spare, channels), w1.dtype)
    w2[:, channels:] = jnp.zeros((w2.shape[0], spare, channels), w2.dtype)

    first = tm * frames
    pair_index = lax.broadcasted_iota(jnp.int32, (1, 1, pairs, 1), 2)

    def put(planes, even, odd, frame_at, row_at):
        nf, nr = even.shape[:2]
        before = jnp.where(pair_index > 0, pltpu.roll(odd, 1, 2), 0.0)
        after = jnp.where(pair_index < pairs - 1, pltpu.roll(even, pairs - 1, 2), 0.0)
        for plane, values in enumerate((before, even, odd, after)):
            planes[plane, pl.ds(frame_at, nf), pl.ds(row_at, nr), :, pl.ds(0, channels)] = (
                values.astype(planes.dtype)
            )

    def frame_valid(shape, frame_at):
        index = first - 2 + frame_at + lax.broadcasted_iota(jnp.int32, shape, 0)
        return index < count

    def put_input(raw, frame_at, row_at):
        nf, nr = raw.shape[:2]
        even, odd = split_pair(raw.astype(jnp.float32), channels)
        valid = frame_valid((nf, 1, 1, 1), frame_at)
        gain = gain1_ref[...].reshape(1, 1, 1, channels)
        put(p1, pair_norm(even, valid, gain), pair_norm(odd, valid, gain), frame_at, row_at)

    def conv(planes, w, frame_at, nf, nr):
        total = None
        for a in range(3):
            for b in range(3):
                for e in range(3):
                    patch = planes[
                        e : e + 2, frame_at + a : frame_at + a + nf, b : b + nr
                    ].reshape(2 * nf * nr * pairs, WIDE)
                    term = jnp.dot(
                        patch, w[(a * 3 + b) * 3 + e], preferred_element_type=jnp.float32
                    )
                    total = term if total is None else total + term
        return total.reshape(2, nf, nr, pairs, channels)

    def hidden(frame_at, nf):
        summed = conv(p1, w1, frame_at, nf, hrows) + bias1_ref[...].reshape(1, 1, 1, 1, channels)
        valid = frame_valid((nf, 1, 1, 1), frame_at + 2)
        if sides == 2:
            row = band * rows - 1 + lax.broadcasted_iota(jnp.int32, (1, hrows, 1, 1), 1)
            valid = valid & (row >= 0) & (row < bands * rows)
        rounded = summed.astype(jnp.bfloat16).astype(jnp.float32)
        gain = gain2_ref[...].reshape(1, 1, 1, channels)
        even = pair_norm(rounded[0], valid, gain)
        odd = pair_norm(rounded[1], valid, gain)
        put(p2, even, odd, frame_at + 2, hidden_at)
        return even, odd

    def finish(frame_at, nf):
        summed = conv(p2, w2, frame_at, nf, rows) + bias2_ref[...].reshape(1, 1, 1, 1, channels)
        joined = jnp.concatenate([summed[0], summed[1]], axis=-1)
        added = joined + x_ref[pl.ds(frame_at, nf)].astype(jnp.float32)
        valid = frame_valid((nf, 1, 1, 1), frame_at + 2)
        out_ref[pl.ds(frame_at, nf)] = jnp.where(valid, added, 0.0).astype(out_ref.dtype)

    for copy in small:
        copy.wait()
    put_input(x_ref[...], 2, own_at)
    for slot, (copy, _, _) in enumerate(space_copies):

        def arrived(slot=slot):
            landed = remote(
                x_ref.at[:, pl.ds(0, 2)], from_space.at[slot], slot, {"space": band}, None, None
            )[0]
            landed.wait_recv()
            put_input(from_space[slot], 2, slot_at[slot])

        when(slot_cond[slot], arrived)

    load1.wait()
    even, odd = hidden(frames - 2, 2)
    hidden_out[0] = even.astype(hidden_out.dtype)
    hidden_out[1] = odd.astype(hidden_out.dtype)
    when(has_next, hidden_copy[0].start)

    def time_arrived():
        time_copy[0].wait_recv()
        put_input(from_time[...], 0, own_at)

    when(has_prev, time_arrived)
    for slot in range(sides):

        def corner_arrived(slot=slot):
            landed = remote(
                x_ref.at[tail, pl.ds(0, 2)],
                from_corner.at[slot],
                2 + slot,
                {"space": band},
                None,
                None,
            )[0]
            landed.wait_recv()
            put_input(from_corner[slot], 0, slot_at[slot])

        when(both(slot_cond[slot], has_prev), corner_arrived)

    hidden(0, frames - 2)
    load2.wait()
    finish(frames - 2, 2)

    def hidden_arrived():
        hidden_copy[0].wait_recv()
        even = hidden_in[0].astype(jnp.float32)
        odd = hidden_in[1].astype(jnp.float32)
        put(p2, even, odd, 0, hidden_at)

    when(has_prev, hidden_arrived)
    finish(0, frames - 2)
    for copy, cond, _ in space_copies + corner_copies + [time_copy, hidden_copy]:
        when(cond, copy.wait_send)


def shards(
    bands,
    blocks,
    latents,
    frame_counts,
    gain_first,
    bias_first,
    weight_first,
    gain_second,
    bias_second,
    weight_second,
):
    channels = gain_first.shape[0]
    frames, rows, flat_width = latents.shape[1:]
    pairs = flat_width // (2 * channels)
    x = latents.reshape(frames, rows, pairs, 2 * channels)
    sides = 1 if bands == 2 else 2
    hrows = rows + sides
    bf16 = jnp.bfloat16
    vmem = pl.BlockSpec(memory_space=pltpu.VMEM)
    hbm = pl.BlockSpec(memory_space=pltpu.HBM)
    out = pl.pallas_call(
        functools.partial(kernel, bands, blocks),
        out_shape=jax.ShapeDtypeStruct(x.shape, bf16),
        in_specs=[pl.BlockSpec(memory_space=pltpu.SMEM)] + [vmem] + [hbm] * 6,
        out_specs=vmem,
        scratch_shapes=[
            pltpu.VMEM((4, 1, channels), jnp.float32),
            pltpu.VMEM((27, WIDE, channels), bf16),
            pltpu.VMEM((27, WIDE, channels), bf16),
            pltpu.VMEM((4, frames + 2, hrows + 2, pairs, WIDE), bf16),
            pltpu.VMEM((4, frames + 2, rows + 2, pairs, WIDE), bf16),
            pltpu.VMEM((2, rows, pairs, 2 * channels), bf16),
            pltpu.VMEM((sides, frames, 2, pairs, 2 * channels), bf16),
            pltpu.VMEM((sides, 2, 2, pairs, 2 * channels), bf16),
            pltpu.VMEM((2, 2, hrows, pairs, channels), bf16),
            pltpu.VMEM((2, 2, hrows, pairs, channels), bf16),
            pltpu.SemaphoreType.DMA((6,)),
            pltpu.SemaphoreType.DMA((6,)),
            pltpu.SemaphoreType.DMA((6,)),
        ],
        compiler_params=pltpu.CompilerParams(
            collective_id=0, has_side_effects=True, vmem_limit_bytes=61 * 1024 * 1024
        ),
    )(
        frame_counts,
        x,
        gain_first.reshape(1, channels),
        bias_first.reshape(1, channels),
        gain_second.reshape(1, channels),
        bias_second.reshape(1, channels),
        weight_first.reshape(27, channels, channels),
        weight_second.reshape(27, channels, channels),
    )
    return out.reshape(latents.shape)


def solution(mesh):
    return jax.shard_map(
        functools.partial(shards, mesh.shape["space"], mesh.shape["tm"]),
        mesh=mesh,
        in_specs=(P(("groups", "clip"), "tm", "space", None), P(("groups", "clip"))) + (P(),) * 6,
        out_specs=P(("groups", "clip"), "tm", "space", None),
        check_vma=False,
    )
```

```python
import functools

import jax
import jax.numpy as jnp
from jax import lax
from jax.experimental import pallas as pl
from jax.experimental.pallas import tpu as pltpu
from jax.sharding import PartitionSpec as P

MESH = pl.DeviceIdType.MESH
WIDE = 256


def pair_norm(values, valid, gain):
    channels = gain.shape[-1]
    mean_square = jnp.sum(values * values, axis=-1, keepdims=True) * (1.0 / channels)
    scaled = values * lax.rsqrt(mean_square + 1e-06) * gain
    out = scaled * jax.nn.sigmoid(scaled)
    return jnp.where(valid, out, 0.0)


def split_pair(flat, channels):
    return flat[..., :channels], flat[..., channels:]


def kernel(
    bands,
    blocks,
    counts_ref,
    x_ref,
    gain1_hbm,
    bias1_hbm,
    gain2_hbm,
    bias2_hbm,
    w1_ref,
    w2_ref,
    out_ref,
    vectors,
    w1,
    w2,
    p1,
    p2,
    from_time,
    from_space,
    from_corner,
    hidden_out,
    hidden_in,
    w_sems,
    send_sems,
    recv_sems,
):
    frames, rows, pairs, flat = x_ref.shape
    channels = flat // 2
    sides = 1 if bands == 2 else 2
    extra = sides
    hrows = rows + extra
    tm = lax.axis_index("tm")
    band = lax.axis_index("space")
    has_prev = tm > 0
    has_next = tm < blocks - 1
    count = counts_ref[0]
    if sides == 1:
        other = 1 - band
        links = [(other, None, other * (rows - 2), 0)]
        own_at = 1 + band
        slot_at = [(1 - band) * (rows + 1)]
        hidden_at = 1 - band
    else:
        links = [
            (band - 1, band > 0, 0, 1),
            (band + 1, band < bands - 1, rows - 2, 0),
        ]
        own_at = 2
        slot_at = [0, rows + 2]
        hidden_at = 0

    def both(a, b):
        return b if a is None else (a if b is None else jnp.logical_and(a, b))

    def when(cond, fn):
        if cond is None:
            fn()
        else:
            pl.when(cond)(fn)

    peers = [({"space": p}, c) for p, c, _, _ in links]
    for step, has in ((1, has_next), (-1, has_prev)):
        peers.append(({"tm": tm + step}, has))
        peers += [({"tm": tm + step, "space": p}, both(c, has)) for p, c, _, _ in links]

    barrier = pltpu.get_barrier_semaphore()
    total = 0
    for device, cond in peers:
        when(
            cond,
            lambda device=device: pl.semaphore_signal(
                barrier, inc=1, device_id=device, device_id_type=MESH
            ),
        )
        total = total + (1 if cond is None else cond.astype(jnp.int32))

    load1 = pltpu.make_async_copy(w1_ref, w1.at[:, pl.ds(0, channels)], w_sems.at[0])
    load2 = pltpu.make_async_copy(w2_ref, w2.at[:, pl.ds(0, channels)], w_sems.at[1])
    small = [
        pltpu.make_async_copy(source, vectors.at[i], w_sems.at[2 + i])
        for i, source in enumerate((gain1_hbm, bias1_hbm, gain2_hbm, bias2_hbm))
    ]
    gain1_ref, bias1_ref, gain2_ref, bias2_ref = [vectors.at[i] for i in range(4)]
    for copy in small:
        copy.start()
    load1.start()
    load2.start()

    p1[...] = jnp.zeros_like(p1)
    p2[...] = jnp.zeros_like(p2)
    spare = WIDE - channels
    w1[:, channels:] = jnp.zeros((w1.shape[0], spare, channels), w1.dtype)
    w2[:, channels:] = jnp.zeros((w2.shape[0], spare, channels), w2.dtype)

    pl.semaphore_wait(barrier, total)

    tail = pl.ds(frames - 2, 2)
    copies = []

    def remote(src, dst, at, device, send_if, recv_if):
        copy = pltpu.make_async_remote_copy(
            src_ref=src,
            dst_ref=dst,
            send_sem=send_sems.at[at],
            recv_sem=recv_sems.at[at],
            device_id=device,
            device_id_type=MESH,
        )
        return copy, send_if, recv_if

    slot_cond = [None] if sides == 1 else [band > 0, band < bands - 1]
    space_copies, corner_copies = [], []
    for peer, cond, edge, slot in links:
        space_copies.append(
            remote(
                x_ref.at[:, pl.ds(edge, 2)], from_space.at[slot], slot, {"space": peer}, cond, None
            )
        )
        corner_copies.append(
            remote(
                x_ref.at[tail, pl.ds(edge, 2)],
                from_corner.at[slot],
                2 + slot,
                {"tm": tm + 1, "space": peer},
                both(cond, has_next),
                None,
            )
        )
    time_copy = remote(x_ref.at[tail], from_time, 4, {"tm": tm + 1}, has_next, has_prev)
    hidden_copy = remote(hidden_out, hidden_in, 5, {"tm": tm + 1}, has_next, has_prev)
    for copy, cond, _ in space_copies + [time_copy] + corner_copies:
        when(cond, copy.start)

    first = tm * frames
    pair_index = lax.broadcasted_iota(jnp.int32, (1, 1, pairs, 1), 2)

    def put(planes, even, odd, frame_at, row_at):
        nf, nr = even.shape[:2]
        before = jnp.where(pair_index > 0, pltpu.roll(odd, 1, 2), 0.0)
        after = jnp.where(pair_index < pairs - 1, pltpu.roll(even, pairs - 1, 2), 0.0)
        for plane, values in enumerate((before, even, odd, after)):
            planes[plane, pl.ds(frame_at, nf), pl.ds(row_at, nr), :, pl.ds(0, channels)] = (
                values.astype(planes.dtype)
            )

    def frame_valid(shape, frame_at):
        index = first - 2 + frame_at + lax.broadcasted_iota(jnp.int32, shape, 0)
        return index < count

    def put_input(raw, frame_at, row_at):
        nf, nr = raw.shape[:2]
        even, odd = split_pair(raw.astype(jnp.float32), channels)
        valid = frame_valid((nf, 1, 1, 1), frame_at)
        gain = gain1_ref[...].reshape(1, 1, 1, channels)
        put(p1, pair_norm(even, valid, gain), pair_norm(odd, valid, gain), frame_at, row_at)

    def conv(planes, w, frame_at, nf, nr):
        total = None
        for a in range(3):
            for b in range(3):
                for e in range(3):
                    patch = planes[
                        e : e + 2, frame_at + a : frame_at + a + nf, b : b + nr
                    ].reshape(2 * nf * nr * pairs, WIDE)
                    term = jnp.dot(
                        patch, w[(a * 3 + b) * 3 + e], preferred_element_type=jnp.float32
                    )
                    total = term if total is None else total + term
        return total.reshape(2, nf, nr, pairs, channels)

    def hidden(frame_at, nf):
        summed = conv(p1, w1, frame_at, nf, hrows) + bias1_ref[...].reshape(1, 1, 1, 1, channels)
        valid = frame_valid((nf, 1, 1, 1), frame_at + 2)
        if sides == 2:
            row = band * rows - 1 + lax.broadcasted_iota(jnp.int32, (1, hrows, 1, 1), 1)
            valid = valid & (row >= 0) & (row < bands * rows)
        rounded = summed.astype(jnp.bfloat16).astype(jnp.float32)
        gain = gain2_ref[...].reshape(1, 1, 1, channels)
        even = pair_norm(rounded[0], valid, gain)
        odd = pair_norm(rounded[1], valid, gain)
        put(p2, even, odd, frame_at + 2, hidden_at)
        return even, odd

    def finish(frame_at, nf):
        summed = conv(p2, w2, frame_at, nf, rows) + bias2_ref[...].reshape(1, 1, 1, 1, channels)
        joined = jnp.concatenate([summed[0], summed[1]], axis=-1)
        added = joined + x_ref[pl.ds(frame_at, nf)].astype(jnp.float32)
        valid = frame_valid((nf, 1, 1, 1), frame_at + 2)
        out_ref[pl.ds(frame_at, nf)] = jnp.where(valid, added, 0.0).astype(out_ref.dtype)

    for copy in small:
        copy.wait()
    put_input(x_ref[...], 2, own_at)
    for slot, (copy, _, _) in enumerate(space_copies):

        def arrived(slot=slot):
            landed = remote(
                x_ref.at[:, pl.ds(0, 2)], from_space.at[slot], slot, {"space": band}, None, None
            )[0]
            landed.wait_recv()
            put_input(from_space[slot], 2, slot_at[slot])

        when(slot_cond[slot], arrived)

    load1.wait()
    even, odd = hidden(frames - 2, 2)
    hidden_out[...] = jnp.concatenate([even, odd], axis=-1).astype(hidden_out.dtype)
    when(has_next, hidden_copy[0].start)

    def time_arrived():
        time_copy[0].wait_recv()
        put_input(from_time[...], 0, own_at)

    when(has_prev, time_arrived)
    for slot in range(sides):

        def corner_arrived(slot=slot):
            landed = remote(
                x_ref.at[tail, pl.ds(0, 2)],
                from_corner.at[slot],
                2 + slot,
                {"space": band},
                None,
                None,
            )[0]
            landed.wait_recv()
            put_input(from_corner[slot], 0, slot_at[slot])

        when(both(slot_cond[slot], has_prev), corner_arrived)

    hidden(0, frames - 2)
    load2.wait()
    finish(frames - 2, 2)

    def hidden_arrived():
        hidden_copy[0].wait_recv()
        even, odd = split_pair(hidden_in[...].astype(jnp.float32), channels)
        put(p2, even, odd, 0, hidden_at)

    when(has_prev, hidden_arrived)
    finish(0, frames - 2)
    for copy, cond, _ in space_copies + corner_copies + [time_copy, hidden_copy]:
        when(cond, copy.wait_send)


def shards(
    bands,
    blocks,
    latents,
    frame_counts,
    gain_first,
    bias_first,
    weight_first,
    gain_second,
    bias_second,
    weight_second,
):
    channels = gain_first.shape[0]
    frames, rows, flat_width = latents.shape[1:]
    pairs = flat_width // (2 * channels)
    x = latents.reshape(frames, rows, pairs, 2 * channels)
    sides = 1 if bands == 2 else 2
    hrows = rows + sides
    bf16 = jnp.bfloat16
    vmem = pl.BlockSpec(memory_space=pltpu.VMEM)
    hbm = pl.BlockSpec(memory_space=pltpu.HBM)
    out = pl.pallas_call(
        functools.partial(kernel, bands, blocks),
        out_shape=pltpu.VMEM(x.shape, bf16),
        in_specs=[pl.BlockSpec(memory_space=pltpu.SMEM)] + [vmem] + [hbm] * 6,
        out_specs=vmem,
        scratch_shapes=[
            pltpu.VMEM((4, 1, channels), jnp.float32),
            pltpu.VMEM((27, WIDE, channels), bf16),
            pltpu.VMEM((27, WIDE, channels), bf16),
            pltpu.VMEM((4, frames + 2, hrows + 2, pairs, WIDE), bf16),
            pltpu.VMEM((4, frames + 2, rows + 2, pairs, WIDE), bf16),
            pltpu.VMEM((2, rows, pairs, 2 * channels), bf16),
            pltpu.VMEM((sides, frames, 2, pairs, 2 * channels), bf16),
            pltpu.VMEM((sides, 2, 2, pairs, 2 * channels), bf16),
            pltpu.VMEM((2, hrows, pairs, 2 * channels), bf16),
            pltpu.VMEM((2, hrows, pairs, 2 * channels), bf16),
            pltpu.SemaphoreType.DMA((6,)),
            pltpu.SemaphoreType.DMA((6,)),
            pltpu.SemaphoreType.DMA((6,)),
        ],
        compiler_params=pltpu.CompilerParams(
            collective_id=0, has_side_effects=True, vmem_limit_bytes=40 * 1024 * 1024
        ),
    )(
        frame_counts,
        pltpu.with_memory_space_constraint(x, pltpu.VMEM),
        pltpu.with_memory_space_constraint(gain_first.reshape(1, channels), pltpu.HBM),
        pltpu.with_memory_space_constraint(bias_first.reshape(1, channels), pltpu.HBM),
        pltpu.with_memory_space_constraint(gain_second.reshape(1, channels), pltpu.HBM),
        pltpu.with_memory_space_constraint(bias_second.reshape(1, channels), pltpu.HBM),
        pltpu.with_memory_space_constraint(weight_first.reshape(27, channels, channels), pltpu.HBM),
        pltpu.with_memory_space_constraint(weight_second.reshape(27, channels, channels), pltpu.HBM),
    )
    return out.reshape(latents.shape)


def solution(mesh):
    return jax.shard_map(
        functools.partial(shards, mesh.shape["space"], mesh.shape["tm"]),
        mesh=mesh,
        in_specs=(P(("groups", "clip"), "tm", "space", None), P(("groups", "clip"))) + (P(),) * 6,
        out_specs=P(("groups", "clip"), "tm", "space", None),
        check_vma=False,
    )
```

```python
import functools

import jax
import jax.numpy as jnp
from jax import lax
from jax.experimental import pallas as pl
from jax.experimental.pallas import tpu as pltpu
from jax.sharding import PartitionSpec as P

MESH = pl.DeviceIdType.MESH
WIDE = 256


def pair_norm(values, valid, gain):
    channels = gain.shape[-1]
    mean_square = jnp.sum(values * values, axis=-1, keepdims=True) * (1.0 / channels)
    scaled = values * lax.rsqrt(mean_square + 1e-06) * gain
    out = scaled * jax.nn.sigmoid(scaled)
    return jnp.where(valid, out, 0.0)


def split_pair(flat, channels):
    return flat[..., :channels], flat[..., channels:]


def kernel(
    bands,
    blocks,
    counts_ref,
    x_ref,
    gain1_hbm,
    bias1_hbm,
    gain2_hbm,
    bias2_hbm,
    w1_ref,
    w2_ref,
    out_ref,
    vectors,
    w1,
    w2,
    p1,
    p2,
    from_time,
    from_space,
    from_corner,
    hidden_out,
    hidden_in,
    w_sems,
    send_sems,
    recv_sems,
):
    frames, rows, pairs, flat = x_ref.shape
    channels = flat // 2
    sides = 1 if bands == 2 else 2
    extra = sides
    hrows = rows + extra
    tm = lax.axis_index("tm")
    band = lax.axis_index("space")
    has_prev = tm > 0
    has_next = tm < blocks - 1
    count = counts_ref[0]
    if sides == 1:
        other = 1 - band
        links = [(other, None, other * (rows - 2), 0)]
        own_at = 1 + band
        slot_at = [(1 - band) * (rows + 1)]
        hidden_at = 1 - band
    else:
        links = [
            (band - 1, band > 0, 0, 1),
            (band + 1, band < bands - 1, rows - 2, 0),
        ]
        own_at = 2
        slot_at = [0, rows + 2]
        hidden_at = 0

    def both(a, b):
        return b if a is None else (a if b is None else jnp.logical_and(a, b))

    def when(cond, fn):
        if cond is None:
            fn()
        else:
            pl.when(cond)(fn)

    peers = [({"space": p}, c) for p, c, _, _ in links]
    for step, has in ((1, has_next), (-1, has_prev)):
        peers.append(({"tm": tm + step}, has))
        peers += [({"tm": tm + step, "space": p}, both(c, has)) for p, c, _, _ in links]

    barrier = pltpu.get_barrier_semaphore()
    total = 0
    for device, cond in peers:
        when(
            cond,
            lambda device=device: pl.semaphore_signal(
                barrier, inc=1, device_id=device, device_id_type=MESH
            ),
        )
        total = total + (1 if cond is None else cond.astype(jnp.int32))

    load1 = pltpu.make_async_copy(w1_ref, w1.at[:, pl.ds(0, channels)], w_sems.at[0])
    load2 = pltpu.make_async_copy(w2_ref, w2.at[:, pl.ds(0, channels)], w_sems.at[1])
    small = [
        pltpu.make_async_copy(source, vectors.at[i], w_sems.at[2 + i])
        for i, source in enumerate((gain1_hbm, bias1_hbm, gain2_hbm, bias2_hbm))
    ]
    gain1_ref, bias1_ref, gain2_ref, bias2_ref = [vectors.at[i] for i in range(4)]
    for copy in small:
        copy.start()
    load1.start()
    load2.start()

    p1[...] = jnp.zeros_like(p1)
    p2[...] = jnp.zeros_like(p2)
    spare = WIDE - channels
    w1[:, channels:] = jnp.zeros((w1.shape[0], spare, channels), w1.dtype)
    w2[:, channels:] = jnp.zeros((w2.shape[0], spare, channels), w2.dtype)

    pl.semaphore_wait(barrier, total)

    tail = pl.ds(frames - 2, 2)
    copies = []

    def remote(src, dst, at, device, send_if, recv_if):
        copy = pltpu.make_async_remote_copy(
            src_ref=src,
            dst_ref=dst,
            send_sem=send_sems.at[at],
            recv_sem=recv_sems.at[at],
            device_id=device,
            device_id_type=MESH,
        )
        return copy, send_if, recv_if

    slot_cond = [None] if sides == 1 else [band > 0, band < bands - 1]
    space_copies, corner_copies = [], []
    for peer, cond, edge, slot in links:
        space_copies.append(
            remote(
                x_ref.at[:, pl.ds(edge, 2)], from_space.at[slot], slot, {"space": peer}, cond, None
            )
        )
        corner_copies.append(
            remote(
                x_ref.at[tail, pl.ds(edge, 2)],
                from_corner.at[slot],
                2 + slot,
                {"tm": tm + 1, "space": peer},
                both(cond, has_next),
                None,
            )
        )
    time_copy = remote(x_ref.at[tail], from_time, 4, {"tm": tm + 1}, has_next, has_prev)
    hidden_copy = remote(hidden_out, hidden_in, 5, {"tm": tm + 1}, has_next, has_prev)
    for copy, cond, _ in space_copies + [time_copy] + corner_copies:
        when(cond, copy.start)

    first = tm * frames
    pair_index = lax.broadcasted_iota(jnp.int32, (1, 1, pairs, 1), 2)

    def put(planes, even, odd, frame_at, row_at):
        nf, nr = even.shape[:2]
        before = jnp.where(pair_index > 0, pltpu.roll(odd, 1, 2), 0.0)
        after = jnp.where(pair_index < pairs - 1, pltpu.roll(even, pairs - 1, 2), 0.0)
        for plane, values in enumerate((before, even, odd, after)):
            planes[plane, pl.ds(frame_at, nf), pl.ds(row_at, nr), :, pl.ds(0, channels)] = (
                values.astype(planes.dtype)
            )

    def frame_valid(shape, frame_at):
        index = first - 2 + frame_at + lax.broadcasted_iota(jnp.int32, shape, 0)
        return index < count

    def put_input(raw, frame_at, row_at):
        nf, nr = raw.shape[:2]
        even, odd = split_pair(raw.astype(jnp.float32), channels)
        valid = frame_valid((nf, 1, 1, 1), frame_at)
        gain = gain1_ref[...].reshape(1, 1, 1, channels)
        put(p1, pair_norm(even, valid, gain), pair_norm(odd, valid, gain), frame_at, row_at)

    def conv(planes, w, frame_at, nf, nr, row_at=0):
        total = None
        for a in range(3):
            for b in range(3):
                for e in range(3):
                    patch = planes[
                        e : e + 2, frame_at + a : frame_at + a + nf, pl.ds(row_at + b, nr)
                    ].reshape(2 * nf * nr * pairs, WIDE)
                    term = jnp.dot(
                        patch, w[(a * 3 + b) * 3 + e], preferred_element_type=jnp.float32
                    )
                    total = term if total is None else total + term
        return total.reshape(2, nf, nr, pairs, channels)

    def hidden(frame_at, nf, nr=hrows, row_at=0):
        summed = conv(p1, w1, frame_at, nf, nr, row_at) + bias1_ref[...].reshape(1, 1, 1, 1, channels)
        valid = frame_valid((nf, 1, 1, 1), frame_at + 2)
        if sides == 2:
            row = band * rows - 1 + lax.broadcasted_iota(jnp.int32, (1, hrows, 1, 1), 1)
            valid = valid & (row >= 0) & (row < bands * rows)
        rounded = summed.astype(jnp.bfloat16).astype(jnp.float32)
        gain = gain2_ref[...].reshape(1, 1, 1, channels)
        even = pair_norm(rounded[0], valid, gain)
        odd = pair_norm(rounded[1], valid, gain)
        put(p2, even, odd, frame_at + 2, hidden_at + row_at)
        return jnp.concatenate([even, odd], axis=-1).astype(hidden_out.dtype)

    def finish(frame_at, nf):
        summed = conv(p2, w2, frame_at, nf, rows) + bias2_ref[...].reshape(1, 1, 1, 1, channels)
        joined = jnp.concatenate([summed[0], summed[1]], axis=-1)
        added = joined + x_ref[pl.ds(frame_at, nf)].astype(jnp.float32)
        valid = frame_valid((nf, 1, 1, 1), frame_at + 2)
        out_ref[pl.ds(frame_at, nf)] = jnp.where(valid, added, 0.0).astype(out_ref.dtype)

    for copy in small:
        copy.wait()
    put_input(x_ref[...], 2, own_at)
    load1.wait()
    if sides == 1:
        near = rows - 1
        hidden_out[:, pl.ds(2 * band, near)] = hidden(frames - 2, 2, near, 2 * band)
    for slot, (copy, _, _) in enumerate(space_copies):

        def arrived(slot=slot):
            landed = remote(
                x_ref.at[:, pl.ds(0, 2)], from_space.at[slot], slot, {"space": band}, None, None
            )[0]
            landed.wait_recv()
            put_input(from_space[slot], 2, slot_at[slot])

        when(slot_cond[slot], arrived)

    if sides == 1:
        far_at = near * (1 - band)
        hidden_out[:, pl.ds(far_at, 2)] = hidden(frames - 2, 2, 2, far_at)
    else:
        hidden_out[...] = hidden(frames - 2, 2)
    when(has_next, hidden_copy[0].start)

    def time_arrived():
        time_copy[0].wait_recv()
        put_input(from_time[...], 0, own_at)

    when(has_prev, time_arrived)
    for slot in range(sides):

        def corner_arrived(slot=slot):
            landed = remote(
                x_ref.at[tail, pl.ds(0, 2)],
                from_corner.at[slot],
                2 + slot,
                {"space": band},
                None,
                None,
            )[0]
            landed.wait_recv()
            put_input(from_corner[slot], 0, slot_at[slot])

        when(both(slot_cond[slot], has_prev), corner_arrived)

    hidden(0, frames - 2)
    load2.wait()
    finish(frames - 2, 2)

    def hidden_arrived():
        hidden_copy[0].wait_recv()
        even, odd = split_pair(hidden_in[...].astype(jnp.float32), channels)
        put(p2, even, odd, 0, hidden_at)

    when(has_prev, hidden_arrived)
    finish(0, frames - 2)
    for copy, cond, _ in space_copies + corner_copies + [time_copy, hidden_copy]:
        when(cond, copy.wait_send)


def shards(
    bands,
    blocks,
    latents,
    frame_counts,
    gain_first,
    bias_first,
    weight_first,
    gain_second,
    bias_second,
    weight_second,
):
    channels = gain_first.shape[0]
    frames, rows, flat_width = latents.shape[1:]
    pairs = flat_width // (2 * channels)
    x = latents.reshape(frames, rows, pairs, 2 * channels)
    sides = 1 if bands == 2 else 2
    hrows = rows + sides
    bf16 = jnp.bfloat16
    vmem = pl.BlockSpec(memory_space=pltpu.VMEM)
    hbm = pl.BlockSpec(memory_space=pltpu.HBM)
    out = pl.pallas_call(
        functools.partial(kernel, bands, blocks),
        out_shape=pltpu.VMEM(x.shape, bf16),
        in_specs=[pl.BlockSpec(memory_space=pltpu.SMEM)] + [vmem] + [hbm] * 6,
        out_specs=vmem,
        scratch_shapes=[
            pltpu.VMEM((4, 1, channels), jnp.float32),
            pltpu.VMEM((27, WIDE, channels), bf16),
            pltpu.VMEM((27, WIDE, channels), bf16),
            pltpu.VMEM((4, frames + 2, hrows + 2, pairs, WIDE), bf16),
            pltpu.VMEM((4, frames + 2, rows + 2, pairs, WIDE), bf16),
            pltpu.VMEM((2, rows, pairs, 2 * channels), bf16),
            pltpu.VMEM((sides, frames, 2, pairs, 2 * channels), bf16),
            pltpu.VMEM((sides, 2, 2, pairs, 2 * channels), bf16),
            pltpu.VMEM((2, hrows, pairs, 2 * channels), bf16),
            pltpu.VMEM((2, hrows, pairs, 2 * channels), bf16),
            pltpu.SemaphoreType.DMA((6,)),
            pltpu.SemaphoreType.DMA((6,)),
            pltpu.SemaphoreType.DMA((6,)),
        ],
        compiler_params=pltpu.CompilerParams(
            collective_id=0, has_side_effects=True, vmem_limit_bytes=40 * 1024 * 1024
        ),
    )(
        frame_counts,
        pltpu.with_memory_space_constraint(x, pltpu.VMEM),
        pltpu.with_memory_space_constraint(gain_first.reshape(1, channels), pltpu.HBM),
        pltpu.with_memory_space_constraint(bias_first.reshape(1, channels), pltpu.HBM),
        pltpu.with_memory_space_constraint(gain_second.reshape(1, channels), pltpu.HBM),
        pltpu.with_memory_space_constraint(bias_second.reshape(1, channels), pltpu.HBM),
        pltpu.with_memory_space_constraint(weight_first.reshape(27, channels, channels), pltpu.HBM),
        pltpu.with_memory_space_constraint(weight_second.reshape(27, channels, channels), pltpu.HBM),
    )
    return out.reshape(latents.shape)


def solution(mesh):
    return jax.shard_map(
        functools.partial(shards, mesh.shape["space"], mesh.shape["tm"]),
        mesh=mesh,
        in_specs=(P(("groups", "clip"), "tm", "space", None), P(("groups", "clip"))) + (P(),) * 6,
        out_specs=P(("groups", "clip"), "tm", "space", None),
        check_vma=False,
    )
```

```python
import functools

import jax
import jax.numpy as jnp
from jax import lax
from jax.experimental import pallas as pl
from jax.experimental.pallas import tpu as pltpu
from jax.sharding import PartitionSpec as P

MESH = pl.DeviceIdType.MESH
WIDE = 256


def pair_norm(values, valid, gain):
    channels = gain.shape[-1]
    mean_square = jnp.sum(values * values, axis=-1, keepdims=True) * (1.0 / channels)
    scaled = values * lax.rsqrt(mean_square + 1e-06) * gain
    out = scaled * jax.nn.sigmoid(scaled)
    return jnp.where(valid, out, 0.0)


def split_pair(flat, channels):
    return flat[..., :channels], flat[..., channels:]


def kernel(
    bands,
    blocks,
    counts_ref,
    x_ref,
    gain1_hbm,
    bias1_hbm,
    gain2_hbm,
    bias2_hbm,
    w1_ref,
    w2_ref,
    out_ref,
    vectors,
    w1,
    w2,
    p1,
    p2,
    from_time,
    from_space,
    from_corner,
    hidden_out,
    hidden_in,
    w_sems,
    send_sems,
    recv_sems,
):
    frames, rows, pairs, flat = x_ref.shape
    channels = flat // 2
    sides = 1 if bands == 2 else 2
    extra = sides
    hrows = rows + extra
    tm = lax.axis_index("tm")
    band = lax.axis_index("space")
    has_prev = tm > 0
    has_next = tm < blocks - 1
    count = counts_ref[0]
    if sides == 1:
        other = 1 - band
        links = [(other, None, other * (rows - 2), 0)]
        own_at = 1 + band
        slot_at = [(1 - band) * (rows + 1)]
        hidden_at = 1 - band
    else:
        links = [
            (band - 1, band > 0, 0, 1),
            (band + 1, band < bands - 1, rows - 2, 0),
        ]
        own_at = 2
        slot_at = [0, rows + 2]
        hidden_at = 0

    def both(a, b):
        return b if a is None else (a if b is None else jnp.logical_and(a, b))

    def when(cond, fn):
        if cond is None:
            fn()
        else:
            pl.when(cond)(fn)

    peers = [({"space": p}, c) for p, c, _, _ in links]
    for step, has in ((1, has_next), (-1, has_prev)):
        peers.append(({"tm": tm + step}, has))
        peers += [({"tm": tm + step, "space": p}, both(c, has)) for p, c, _, _ in links]

    barrier = pltpu.get_barrier_semaphore()
    total = 0
    for device, cond in peers:
        when(
            cond,
            lambda device=device: pl.semaphore_signal(
                barrier, inc=1, device_id=device, device_id_type=MESH
            ),
        )
        total = total + (1 if cond is None else cond.astype(jnp.int32))

    load1 = pltpu.make_async_copy(w1_ref, w1.at[:, pl.ds(0, channels)], w_sems.at[0])
    load2 = pltpu.make_async_copy(w2_ref, w2.at[:, pl.ds(0, channels)], w_sems.at[1])
    small = [
        pltpu.make_async_copy(source, vectors.at[i], w_sems.at[2 + i])
        for i, source in enumerate((gain1_hbm, bias1_hbm, gain2_hbm, bias2_hbm))
    ]
    gain1_ref, bias1_ref, gain2_ref, bias2_ref = [vectors.at[i] for i in range(4)]
    for copy in small:
        copy.start()
    load1.start()
    load2.start()

    p1[...] = jnp.zeros_like(p1)
    p2[...] = jnp.zeros_like(p2)
    spare = WIDE - channels
    w1[:, channels:] = jnp.zeros((w1.shape[0], spare, channels), w1.dtype)
    w2[:, channels:] = jnp.zeros((w2.shape[0], spare, channels), w2.dtype)

    pl.semaphore_wait(barrier, total)

    tail = pl.ds(frames - 2, 2)
    copies = []

    def remote(src, dst, at, device, send_if, recv_if):
        copy = pltpu.make_async_remote_copy(
            src_ref=src,
            dst_ref=dst,
            send_sem=send_sems.at[at],
            recv_sem=recv_sems.at[at],
            device_id=device,
            device_id_type=MESH,
        )
        return copy, send_if, recv_if

    slot_cond = [None] if sides == 1 else [band > 0, band < bands - 1]
    space_copies, corner_copies = [], []
    for peer, cond, edge, slot in links:
        space_copies.append(
            remote(
                x_ref.at[:, pl.ds(edge, 2)], from_space.at[slot], slot, {"space": peer}, cond, None
            )
        )
        corner_copies.append(
            remote(
                x_ref.at[tail, pl.ds(edge, 2)],
                from_corner.at[slot],
                2 + slot,
                {"tm": tm + 1, "space": peer},
                both(cond, has_next),
                None,
            )
        )
    time_copy = remote(x_ref.at[tail], from_time, 4, {"tm": tm + 1}, has_next, has_prev)
    hidden_copy = remote(hidden_out, hidden_in, 5, {"tm": tm + 1}, has_next, has_prev)
    for copy, cond, _ in space_copies + [time_copy] + corner_copies:
        when(cond, copy.start)

    first = tm * frames
    pair_index = lax.broadcasted_iota(jnp.int32, (1, 1, pairs, 1), 2)

    def put(planes, even, odd, frame_at, row_at):
        nf, nr = even.shape[:2]
        before = jnp.where(pair_index > 0, pltpu.roll(odd, 1, 2), 0.0)
        after = jnp.where(pair_index < pairs - 1, pltpu.roll(even, pairs - 1, 2), 0.0)
        for plane, values in enumerate((before, even, odd, after)):
            planes[plane, pl.ds(frame_at, nf), pl.ds(row_at, nr), :, pl.ds(0, channels)] = (
                values.astype(planes.dtype)
            )

    def frame_valid(shape, frame_at):
        index = first - 2 + frame_at + lax.broadcasted_iota(jnp.int32, shape, 0)
        return index < count

    def put_input(raw, frame_at, row_at):
        nf, nr = raw.shape[:2]
        even, odd = split_pair(raw.astype(jnp.float32), channels)
        valid = frame_valid((nf, 1, 1, 1), frame_at)
        gain = gain1_ref[...].reshape(1, 1, 1, channels)
        put(p1, pair_norm(even, valid, gain), pair_norm(odd, valid, gain), frame_at, row_at)

    def conv(planes, w, frame_at, nf, nr, row_at=0):
        total = None
        for a in range(3):
            for b in range(3):
                for e in range(3):
                    patch = planes[
                        e : e + 2, frame_at + a : frame_at + a + nf, pl.ds(row_at + b, nr)
                    ].reshape(2 * nf * nr * pairs, WIDE)
                    term = jnp.dot(
                        patch, w[(a * 3 + b) * 3 + e], preferred_element_type=jnp.float32
                    )
                    total = term if total is None else total + term
        return total.reshape(2, nf, nr, pairs, channels)

    def hidden(frame_at, nf, nr=hrows, row_at=0):
        summed = conv(p1, w1, frame_at, nf, nr, row_at) + bias1_ref[...].reshape(1, 1, 1, 1, channels)
        valid = frame_valid((nf, 1, 1, 1), frame_at + 2)
        if sides == 2:
            row = band * rows - 1 + lax.broadcasted_iota(jnp.int32, (1, hrows, 1, 1), 1)
            valid = valid & (row >= 0) & (row < bands * rows)
        rounded = summed.astype(jnp.bfloat16).astype(jnp.float32)
        gain = gain2_ref[...].reshape(1, 1, 1, channels)
        even = pair_norm(rounded[0], valid, gain)
        odd = pair_norm(rounded[1], valid, gain)
        put(p2, even, odd, frame_at + 2, hidden_at + row_at)
        return jnp.concatenate([even, odd], axis=-1).astype(hidden_out.dtype)

    def finish(frame_at, nf):
        summed = conv(p2, w2, frame_at, nf, rows) + bias2_ref[...].reshape(1, 1, 1, 1, channels)
        joined = jnp.concatenate([summed[0], summed[1]], axis=-1)
        added = joined + x_ref[pl.ds(frame_at, nf)].astype(jnp.float32)
        valid = frame_valid((nf, 1, 1, 1), frame_at + 2)
        out_ref[pl.ds(frame_at, nf)] = jnp.where(valid, added, 0.0).astype(out_ref.dtype)

    for copy in small:
        copy.wait()
    put_input(x_ref[...], 2, own_at)
    load1.wait()
    if sides == 1:
        near = rows - 1
        hidden_out[:, pl.ds(2 * band, near)] = hidden(frames - 2, 2, near, 2 * band)
    for slot, (copy, _, _) in enumerate(space_copies):

        def arrived(slot=slot):
            landed = remote(
                x_ref.at[:, pl.ds(0, 2)], from_space.at[slot], slot, {"space": band}, None, None
            )[0]
            landed.wait_recv()
            put_input(from_space[slot], 2, slot_at[slot])

        when(slot_cond[slot], arrived)

    if sides == 1:
        far_at = near * (1 - band)
        hidden_out[:, pl.ds(far_at, 2)] = hidden(frames - 2, 2, 2, far_at)
    else:
        hidden_out[...] = hidden(frames - 2, 2)
    when(has_next, hidden_copy[0].start)

    def time_arrived():
        time_copy[0].wait_recv()
        put_input(from_time[...], 0, own_at)

    when(has_prev, time_arrived)
    if sides == 1:
        hidden(0, frames - 2, near, 2 * band)
    for slot in range(sides):

        def corner_arrived(slot=slot):
            landed = remote(
                x_ref.at[tail, pl.ds(0, 2)],
                from_corner.at[slot],
                2 + slot,
                {"space": band},
                None,
                None,
            )[0]
            landed.wait_recv()
            put_input(from_corner[slot], 0, slot_at[slot])

        when(both(slot_cond[slot], has_prev), corner_arrived)

    if sides == 1:
        hidden(0, frames - 2, 2, far_at)
    else:
        hidden(0, frames - 2)
    load2.wait()
    finish(frames - 2, 2)

    def hidden_arrived():
        hidden_copy[0].wait_recv()
        even, odd = split_pair(hidden_in[...].astype(jnp.float32), channels)
        put(p2, even, odd, 0, hidden_at)

    when(has_prev, hidden_arrived)
    finish(0, frames - 2)
    for copy, cond, _ in space_copies + corner_copies + [time_copy, hidden_copy]:
        when(cond, copy.wait_send)


def shards(
    bands,
    blocks,
    latents,
    frame_counts,
    gain_first,
    bias_first,
    weight_first,
    gain_second,
    bias_second,
    weight_second,
):
    channels = gain_first.shape[0]
    frames, rows, flat_width = latents.shape[1:]
    pairs = flat_width // (2 * channels)
    x = latents.reshape(frames, rows, pairs, 2 * channels)
    sides = 1 if bands == 2 else 2
    hrows = rows + sides
    bf16 = jnp.bfloat16
    vmem = pl.BlockSpec(memory_space=pltpu.VMEM)
    hbm = pl.BlockSpec(memory_space=pltpu.HBM)
    out = pl.pallas_call(
        functools.partial(kernel, bands, blocks),
        out_shape=pltpu.VMEM(x.shape, bf16),
        in_specs=[pl.BlockSpec(memory_space=pltpu.SMEM)] + [vmem] + [hbm] * 6,
        out_specs=vmem,
        scratch_shapes=[
            pltpu.VMEM((4, 1, channels), jnp.float32),
            pltpu.VMEM((27, WIDE, channels), bf16),
            pltpu.VMEM((27, WIDE, channels), bf16),
            pltpu.VMEM((4, frames + 2, hrows + 2, pairs, WIDE), bf16),
            pltpu.VMEM((4, frames + 2, rows + 2, pairs, WIDE), bf16),
            pltpu.VMEM((2, rows, pairs, 2 * channels), bf16),
            pltpu.VMEM((sides, frames, 2, pairs, 2 * channels), bf16),
            pltpu.VMEM((sides, 2, 2, pairs, 2 * channels), bf16),
            pltpu.VMEM((2, hrows, pairs, 2 * channels), bf16),
            pltpu.VMEM((2, hrows, pairs, 2 * channels), bf16),
            pltpu.SemaphoreType.DMA((6,)),
            pltpu.SemaphoreType.DMA((6,)),
            pltpu.SemaphoreType.DMA((6,)),
        ],
        compiler_params=pltpu.CompilerParams(
            collective_id=0, has_side_effects=True, vmem_limit_bytes=40 * 1024 * 1024
        ),
    )(
        frame_counts,
        pltpu.with_memory_space_constraint(x, pltpu.VMEM),
        pltpu.with_memory_space_constraint(gain_first.reshape(1, channels), pltpu.HBM),
        pltpu.with_memory_space_constraint(bias_first.reshape(1, channels), pltpu.HBM),
        pltpu.with_memory_space_constraint(gain_second.reshape(1, channels), pltpu.HBM),
        pltpu.with_memory_space_constraint(bias_second.reshape(1, channels), pltpu.HBM),
        pltpu.with_memory_space_constraint(weight_first.reshape(27, channels, channels), pltpu.HBM),
        pltpu.with_memory_space_constraint(weight_second.reshape(27, channels, channels), pltpu.HBM),
    )
    return out.reshape(latents.shape)


def solution(mesh):
    return jax.shard_map(
        functools.partial(shards, mesh.shape["space"], mesh.shape["tm"]),
        mesh=mesh,
        in_specs=(P(("groups", "clip"), "tm", "space", None), P(("groups", "clip"))) + (P(),) * 6,
        out_specs=P(("groups", "clip"), "tm", "space", None),
        check_vma=False,
    )
```
